512 devices in a mesh: win: 16 (over x, y), tile: 32 (over z, core).
Axes of the slice: x: 4, y: 4, z: 16, core: 2. Of those that a mesh axis runs over, the one named last changes fastest.
Arguments:
- multiplier: float32 [16, 72, 256, 128], P('win', None, 'tile'), may hold values from -6 to 6
- coef_diag: float32 [16, 72, 256, 128], P('win', None, 'tile'), may hold values from 0.2 to 0.6
- coef_side: float32 [16, 72, 256, 128], P('win', None, 'tile'), may hold values from 0.05 to 0.15
- mixing: float32 [72, 72], replicated, may hold values from -0.75 to 0.75
- jacobians: bfloat16 [8, 72, 128], replicated, may hold values from -0.5 to 0.5
- departures: bfloat16 [16, 2, 65536, 128], P('win', None, 'tile'), may hold values from -6 to 6
- counts: int32 [16, 2, 32, 32], P('win', None, 'tile'), may hold values from 0 to 128, as said below
- row_order: int32 [16, 2, 32, 2048], P('win', None, 'tile'), may hold values from 0 to 2047, each once within a row
- obs_cell: int32 [16, 2, 65536], P('win', None, 'tile'), may hold values from 0 to 1023
- obs_block: int32 [16, 2, 65536], P('win', None, 'tile'), may hold values from 0 to 7
Outputs:
- state_adjoint: float32 [16, 72, 256, 128], P('win', None, 'tile')
The draws below stay inside these ranges and needn't reach their ends.
Inputs may be any that keep to these rules, and one draw needn't show every extreme that they name: Each owner's counts at one time sum to at most 2048; in every sub-window and time some tile receives 128 rows from every owner.
All inputs are finite; a program needn't handle non-finite values.
Results may differ from the reference program's by a relative error of at most 0.0022.
Values may be sent and summed in bfloat16 or wider, within the bound.
No kernel may reach another device: no remote copies, remote signals or barrier semaphores. Data moves between devices by JAX's collectives and lax.ppermute only.
A program may use at most 64 MiB of HBM per device.

```python
from functools import partial
import jax
import jax.numpy as jnp
from jax import lax

C = 72
NCH = 128
NBLK = 8
LAT = 128
CAP = 128
WINDOWS = 16
TILES = 32
NLON = 256
CELLS = 1024
ROWS_DEV = 2048
ROWS_ALL = 65536


def draw_counts(key, part):
    key = jax.random.fold_in(key, 7)
    rank_key, crowd_key, sparse_key = jax.random.split(key, 3)
    ranking = jax.random.permutation(rank_key, TILES)
    grid_shape = (WINDOWS, 2, TILES, TILES)
    crowded = jax.random.randint(crowd_key, grid_shape, CAP // 2, CAP + 1)
    sparse_vals = jax.random.randint(sparse_key, grid_shape, 0, CAP // 4 + 1)
    drawn = jnp.where(ranking < TILES // 4, crowded, sparse_vals)
    return jnp.where(ranking == 0, CAP, drawn).astype(jnp.int32)


def with_ends(values, rng, least, largest):
    place = [jax.random.randint(jax.random.fold_in(rng, axis), (), 0, length) for axis, length in enumerate(values.shape)]
    main_axis = values.shape.index(max(values.shape))
    neighbour = place[:main_axis] + [(place[main_axis] + 1) % values.shape[main_axis]] + place[main_axis + 1:]
    return values.at[tuple(place)].set(least).at[tuple(neighbour)].set(largest)


def level_of(own_key, extent, pieces, smallest, top_value):
    gain, own = 1.0, jax.random.fold_in(own_key, 6)
    for dim, parts in pieces:
        draws = jnp.exp(jax.random.uniform(jax.random.fold_in(own, dim), (parts,), jnp.float32, smallest / len(pieces), top_value / len(pieces)))
        gain = gain * jnp.repeat(draws, extent[dim] // parts).reshape([-1 if axis == dim else 1 for axis in range(len(extent))])
    return gain


def noise(stream_key, dims, deviation, reach, pieces=(), held_as=jnp.bfloat16):
    result = deviation * jax.random.normal(stream_key, dims, jnp.float32)
    if pieces:
        result = result * level_of(stream_key, dims, pieces, -0.22, 0.18)
    return jnp.clip(result, -reach, reach).astype(held_as)


def setup_inputs(seed: int = 0) -> dict:
    splits = jax.random.split(jax.random.key(seed), 11)
    multiplier = noise(splits[0], (WINDOWS, C, NLON, LAT), 1.0, 6.0, ((0, 16), (2, 32)), jnp.float32)
    coef_diag = jnp.clip(0.2 + 0.400000021 * jax.random.uniform(splits[1], (WINDOWS, C, NLON, LAT), jnp.float32) ** level_of(splits[1], (WINDOWS, C, NLON, LAT), ((0, 16), (2, 32)), -0.2, 0.2), 0.2, 0.6)
    coef_side = jnp.clip(0.05 + 0.10000001 * jax.random.uniform(splits[2], (WINDOWS, C, NLON, LAT), jnp.float32) ** level_of(splits[2], (WINDOWS, C, NLON, LAT), ((0, 16), (2, 32)), -0.2, 0.2), 0.05, 0.15)
    mixing = noise(splits[3], (C, C), C ** -0.5, 0.75, (), jnp.float32)
    jacobians = noise(splits[4], (NBLK, C, NCH), NCH ** -0.5, 0.5)
    departures = noise(splits[5], (WINDOWS, 2, ROWS_ALL, NCH), 1.0, 6.0, ((0, 16), (2, 32)))
    counts = draw_counts(jax.random.fold_in(splits[10], 71), 0)
    row_order = jax.vmap(lambda own: jax.random.permutation(own, ROWS_DEV))(jax.random.split(splits[7], WINDOWS * 2 * TILES)).reshape((WINDOWS, 2, TILES, ROWS_DEV)).astype(jnp.int32)
    obs_cell = with_ends(jax.random.randint(splits[8], (WINDOWS, 2, ROWS_ALL), 0, CELLS), jax.random.fold_in(splits[8], 1), 0, CELLS - 1).astype(jnp.int32)
    obs_block = with_ends(jax.random.randint(splits[9], (WINDOWS, 2, ROWS_ALL), 0, NBLK), jax.random.fold_in(splits[9], 1), 0, NBLK - 1).astype(jnp.int32)
    return dict(multiplier=multiplier, coef_diag=coef_diag, coef_side=coef_side, mixing=mixing, jacobians=jacobians, departures=departures, counts=counts, row_order=row_order, obs_cell=obs_cell, obs_block=obs_block)


def adjoint_step(state_in, coef_diag, coef_side, mixing):
    mixed = jnp.einsum("cd,wcxy->wdxy", mixing, state_in, precision=lax.Precision.HIGHEST)
    east_west = jnp.roll(mixed, 1, axis=2) + jnp.roll(mixed, -1, axis=2)
    padded = jnp.pad(mixed, ((0, 0), (0, 0), (0, 0), (1, 1)))
    return coef_diag * mixed + coef_side * (east_west + padded[..., 2:] + padded[..., :-2])


def obs_adjoint(items, jacobians):
    rows_in, tile_counts, row_order, cell_ids, block_ids = items
    product_all = jnp.zeros((rows_in.shape[0], jacobians.shape[1]), jnp.float32)
    for block in range(NBLK):
        product = jnp.dot(rows_in, jacobians[block].T, preferred_element_type=jnp.float32)
        product_all = jnp.where(block_ids[:, None] == block, product, product_all)
    values = product_all.astype(jnp.bfloat16)
    row_ends = jnp.cumsum(tile_counts, axis=1).astype(jnp.int32)
    positions = jnp.arange(ROWS_DEV, dtype=jnp.int32)
    destination = jnp.sum((positions[None, :, None] >= row_ends[:, None, :]).astype(jnp.int32), axis=2).astype(jnp.int32)
    is_live = (positions[None, :] < row_ends[:, -1:]).reshape(-1)
    row_ids = (jnp.arange(TILES, dtype=jnp.int32)[:, None] * ROWS_DEV + row_order).astype(jnp.int32).reshape(-1)
    global_cell = jnp.where(is_live, destination.reshape(-1) * CELLS + cell_ids[row_ids], 0).astype(jnp.int32)
    chosen = jnp.where(is_live[:, None], values[row_ids].astype(jnp.float32), 0.0)
    summed = jax.ops.segment_sum(chosen, global_cell, num_segments=NLON * LAT)
    return summed.T.reshape(C, NLON, LAT)


def reference(multiplier, coef_diag, coef_side, mixing, jacobians, departures, counts, row_order, obs_cell, obs_block):
    items = (departures.reshape(WINDOWS * 2, ROWS_ALL, NCH), counts.reshape(WINDOWS * 2, TILES, TILES), row_order.reshape(WINDOWS * 2, TILES, ROWS_DEV), obs_cell.reshape(WINDOWS * 2, ROWS_ALL), obs_block.reshape(WINDOWS * 2, ROWS_ALL))
    adj_obs = lax.map(partial(obs_adjoint, jacobians=jacobians), items).reshape(WINDOWS, 2, C, NLON, LAT)
    following = jnp.concatenate([multiplier[1:], jnp.zeros_like(multiplier[:1])], axis=0)
    first_step = adjoint_step(following, coef_diag, coef_side, mixing)
    second = adjoint_step(adj_obs[:, 1] - first_step, coef_diag, coef_side, mixing)
    return multiplier + adj_obs[:, 0] + second
```

```python
import jax
import jax.numpy as jnp
from jax import lax
from jax.experimental import pallas as pl
from jax.experimental.pallas import tpu as pltpu
from jax.sharding import PartitionSpec as P

CAP = 128
LO = 256
META = 8
F32 = jnp.float32
BF16 = jnp.bfloat16
NT = (((1,), (1,)), ((), ()))
VMEM = pl.BlockSpec(memory_space=pltpu.VMEM)
SMEM = pl.BlockSpec(memory_space=pltpu.SMEM)
PARAMS = pltpu.CompilerParams(vmem_limit_bytes=48 * 2**20)


def pack_kernel(counts, deps, order, cells, blocks, jac, wire, listed):
    kinds, width, _ = jac.shape
    tiles = wire.shape[0]
    rows = deps.shape[2]
    parts = rows // LO
    high = width + META
    jac_all = jnp.concatenate([jac[b].astype(F32) for b in range(kinds)], axis=0).astype(BF16)
    meta_row = lax.broadcasted_iota(jnp.int32, (META, LO), 0)
    sub = lax.broadcasted_iota(jnp.int32, (LO, LO), 0)
    for m in range(2):
        pieces = []
        for j in range(parts):
            span = slice(j * LO, (j + 1) * LO)
            prod = lax.dot_general(jac_all, deps[0, m, span, :], NT, preferred_element_type=F32)
            kind = blocks[0, m : m + 1, span]
            vals = prod[:width]
            for b in range(1, kinds):
                vals = jnp.where(kind == b, prod[b * width : (b + 1) * width], vals)
            cell = cells[0, m : m + 1, span]
            meta = jnp.where(meta_row == 2 * m, cell >> 8, 0)
            meta = jnp.where(meta_row == 2 * m + 1, cell & (LO - 1), meta)
            pieces.append(jnp.concatenate([vals, meta.astype(F32)], axis=0).astype(BF16))
        stacked = jnp.concatenate(pieces, axis=0)
        for n in range(parts):
            want = order[0, m, :, n * LO : (n + 1) * LO]
            onehot = (sub == (want & (LO - 1))).astype(F32).astype(BF16)
            both = jnp.dot(stacked, onehot, preferred_element_type=F32)
            part = want >> 8
            got = both[:high]
            for h in range(1, parts):
                got = jnp.where(part == h, both[h * high : (h + 1) * high], got)
            listed[m, 2 * n] = got[:, :CAP]
            listed[m, 2 * n + 1] = got[:, CAP:]
        listed[m, 2 * parts] = jnp.zeros((high, CAP), F32)
        listed[m, 2 * parts + 1] = jnp.zeros((high, CAP), F32)

    lane = lax.broadcasted_iota(jnp.int32, (high, CAP), 1)
    meta_lane = lax.broadcasted_iota(jnp.int32, (META, CAP), 1)
    meta_sub = lax.broadcasted_iota(jnp.int32, (META, CAP), 0)

    def window(m, start):
        base = start >> 7
        shift = start & (CAP - 1)
        back = (CAP - shift) & (CAP - 1)
        near = pltpu.roll(listed[m, base], back, 1)
        far = pltpu.roll(listed[m, base + 1], back, 1)
        return jnp.where(lane < CAP - shift, near, far)

    def cut(q, starts):
        sizes = [counts[0, m, 0, q] for m in range(2)]
        got = [window(m, starts[m]) for m in range(2)]
        meta = [jnp.where(meta_lane < sizes[m], got[m][width:], -1.0) for m in range(2)]
        meta = jnp.where(meta_sub < 2, meta[0], meta[1])
        wire[q] = jnp.concatenate([got[0][:width], meta, got[1][:width]], axis=0).astype(BF16)
        return tuple(starts[m] + sizes[m] for m in range(2))

    lax.fori_loop(0, tiles, cut, (jnp.int32(0), jnp.int32(0)))


def scatter(wire, m, width):
    tiles = wire.shape[0]
    group = 4
    lanes = group * CAP
    low = lax.broadcasted_iota(jnp.int32, (LO, lanes), 0)
    first = 0 if m == 0 else width + META
    total = None
    for s in range(0, tiles, group):
        vals = [wire[s + i, first : first + width, :].astype(F32) for i in range(group)]
        meta = [wire[s + i, width - META : width + META, :].astype(F32) for i in range(group)]
        vals = jnp.concatenate(vals, axis=1)
        meta = jnp.concatenate(meta, axis=1).astype(jnp.int32)
        cell_hi = meta[META + 2 * m : META + 2 * m + 1]
        cell_lo = meta[META + 2 * m + 1 : META + 2 * m + 2]
        split = [jnp.where(cell_hi == h, vals, 0.0) for h in range(4)]
        left = jnp.concatenate(split, axis=0).astype(BF16)
        right = (low == cell_lo).astype(F32).astype(BF16)
        part = lax.dot_general(left, right, NT, preferred_element_type=F32)
        total = part if total is None else total + part
    return total


def mixed_kernel(wire, first_step, mix_t, mixed, west, east):
    width = mix_t.shape[0]
    total = scatter(wire, 1, width)
    mix = mix_t[...]
    mix_hi = mix.astype(BF16)
    mix_lo = (mix - mix_hi.astype(F32)).astype(BF16)
    for h in range(4):
        start = jnp.concatenate([first_step[2 * h], first_step[2 * h + 1]], axis=1)
        field = total[h * width : (h + 1) * width] - start
        field_hi = field.astype(BF16)
        field_lo = (field - field_hi.astype(F32)).astype(BF16)
        out = jnp.dot(mix_hi, field_hi, preferred_element_type=F32)
        out += jnp.dot(mix_hi, field_lo, preferred_element_type=F32)
        out += jnp.dot(mix_lo, field_hi, preferred_element_type=F32)
        mixed[2 * h] = out[:, :CAP]
        mixed[2 * h + 1] = out[:, CAP:]
        if h == 0:
            west[...] = out[:, :CAP]
        if h == 3:
            east[...] = out[:, CAP:]


def direct_kernel(wire, multiplier, base):
    width = multiplier.shape[1]
    total = scatter(wire, 0, width)
    for h in range(4):
        part = total[h * width : (h + 1) * width]
        base[2 * h] = multiplier[2 * h] + part[:, :CAP]
        base[2 * h + 1] = multiplier[2 * h + 1] + part[:, CAP:]


def final_kernel(mixed, west, east, diag, side, base, out):
    lons, width, lats = mixed.shape
    lane = lax.broadcasted_iota(jnp.int32, (width, lats), 1)
    rows = []
    for i in range(lons):
        here = mixed[i]
        beside = (mixed[i - 1] if i else west[...]) + (mixed[i + 1] if i + 1 < lons else east[...])
        north = jnp.where(lane == lats - 1, 0.0, pltpu.roll(here, lats - 1, 1))
        south = jnp.where(lane == 0, 0.0, pltpu.roll(here, 1, 1))
        rows.append(base[i] + diag[i] * here + side[i] * (beside + north + south))
    out[...] = jnp.stack(rows, axis=1)


def halo(first, last):
    count = lax.axis_size("tile")
    up = [(i, (i + 1) % count) for i in range(count)]
    down = [(j, i) for i, j in up]
    return lax.ppermute(last, "tile", up), lax.ppermute(first, "tile", down)


def local(
    multiplier,
    coef_diag,
    coef_side,
    mixing,
    jacobians,
    departures,
    counts,
    row_order,
    obs_cell,
    obs_block,
):
    tiles = lax.axis_size("tile")
    _, width, lons, lats = multiplier.shape
    rows = departures.shape[2]
    high = 2 * width + META
    wire = pl.pallas_call(
        pack_kernel,
        out_shape=jax.ShapeDtypeStruct((tiles, high, CAP), BF16),
        in_specs=[SMEM] + [VMEM] * 5,
        out_specs=VMEM,
        scratch_shapes=[pltpu.VMEM((2, rows // CAP + 2, width + META, CAP), F32)],
        compiler_params=PARAMS,
        name="pack",
    )(counts, departures, row_order, obs_cell, obs_block, jacobians)
    wire, multiplier, coef_diag, coef_side, mixing = lax.optimization_barrier(
        (wire, multiplier, coef_diag, coef_side, mixing)
    )
    received = lax.all_to_all(wire, "tile", split_axis=0, concat_axis=0, tiled=True)

    mult_t = multiplier[0].transpose(1, 0, 2)
    diag_t = coef_diag[0].transpose(1, 0, 2)
    side_t = coef_side[0].transpose(1, 0, 2)
    mix_t = mixing.T
    windows = lax.axis_size("win")
    following = lax.ppermute(
        mult_t.astype(BF16), "win", [(i, i - 1) for i in range(1, windows)]
    ).astype(F32)
    mixed = jnp.einsum("cd,xcy->xdy", mixing, following, precision=lax.Precision.HIGHEST)
    west, east = halo(mixed[0], mixed[-1])
    rimmed = jnp.concatenate([west[None], mixed, east[None]], axis=0)
    padded = jnp.pad(mixed, ((0, 0), (0, 0), (1, 1)))
    beside = rimmed[2:] + rimmed[:-2] + padded[:, :, 2:] + padded[:, :, :-2]
    first_step = diag_t * mixed + side_t * beside

    field = jax.ShapeDtypeStruct((lons, width, lats), F32)
    edge = jax.ShapeDtypeStruct((width, lats), F32)
    mixed, first, last = pl.pallas_call(
        mixed_kernel,
        out_shape=(field, edge, edge),
        in_specs=[VMEM] * 3,
        out_specs=(VMEM,) * 3,
        compiler_params=PARAMS,
        name="mix",
    )(received, first_step, mix_t)
    west, east = halo(first, last)
    base = pl.pallas_call(
        direct_kernel,
        out_shape=field,
        in_specs=[VMEM] * 2,
        out_specs=VMEM,
        compiler_params=PARAMS,
        name="direct",
    )(received, mult_t)
    out = pl.pallas_call(
        final_kernel,
        out_shape=jax.ShapeDtypeStruct((width, lons, lats), F32),
        in_specs=[VMEM] * 6,
        out_specs=VMEM,
        compiler_params=PARAMS,
        name="final",
    )(mixed, west, east, diag_t, side_t, base)
    return out[None]


def solution(mesh):
    in_specs = (
        P("win", None, "tile", None),
        P("win", None, "tile", None),
        P("win", None, "tile", None),
        P(),
        P(),
        P("win", None, "tile", None),
        P("win", None, "tile", None),
        P("win", None, "tile", None),
        P("win", None, "tile"),
        P("win", None, "tile"),
    )
    out_specs = P("win", None, "tile", None)
    return jax.shard_map(local, mesh=mesh, in_specs=in_specs, out_specs=out_specs, check_vma=False)
```

```python
import jax
import jax.numpy as jnp
from jax import lax
from jax.experimental import pallas as pl
from jax.experimental.pallas import tpu as pltpu
from jax.sharding import PartitionSpec as P

CAP = 128
LO = 256
META = 8
F32 = jnp.float32
BF16 = jnp.bfloat16
NT = (((1,), (1,)), ((), ()))
VMEM = pl.BlockSpec(memory_space=pltpu.VMEM)
HBM = pl.BlockSpec(memory_space=pltpu.HBM)
SMEM = pl.BlockSpec(memory_space=pltpu.SMEM)
PARAMS = pltpu.CompilerParams(vmem_limit_bytes=48 * 2**20)
PACK_PARAMS = pltpu.CompilerParams(vmem_limit_bytes=60 * 2**20)


def pack_kernel(
    counts_hbm,
    deps_hbm,
    order_hbm,
    cells_hbm,
    blocks_hbm,
    jac_hbm,
    wire,
    counts,
    deps,
    order,
    cells,
    blocks,
    jac,
    listed,
    sems,
):
    loads = [
        pltpu.make_async_copy(jac_hbm, jac, sems.at[0]),
        pltpu.make_async_copy(blocks_hbm, blocks, sems.at[1]),
        pltpu.make_async_copy(cells_hbm, cells, sems.at[2]),
        pltpu.make_async_copy(deps_hbm.at[0, 0], deps.at[0], sems.at[3]),
        pltpu.make_async_copy(order_hbm, order, sems.at[4]),
        pltpu.make_async_copy(deps_hbm.at[0, 1], deps.at[1], sems.at[5]),
        pltpu.make_async_copy(counts_hbm, counts, sems.at[6]),
    ]
    for load in loads:
        load.start()
    kinds, width, _ = jac.shape
    tiles = wire.shape[0]
    rows = deps.shape[1]
    parts = rows // LO
    high = width + META
    meta_row = lax.broadcasted_iota(jnp.int32, (META, LO), 0)
    sub = lax.broadcasted_iota(jnp.int32, (LO, LO), 0)
    for load in loads[:4]:
        load.wait()
    jac_all = jnp.concatenate([jac[b].astype(F32) for b in range(kinds)], axis=0).astype(BF16)
    for m in range(2):
        if m:
            loads[5].wait()
        pieces = []
        for j in range(parts):
            span = slice(j * LO, (j + 1) * LO)
            prod = lax.dot_general(jac_all, deps[m, span, :], NT, preferred_element_type=F32)
            kind = blocks[0, m : m + 1, span]
            vals = prod[:width]
            for b in range(1, kinds):
                vals = jnp.where(kind == b, prod[b * width : (b + 1) * width], vals)
            cell = cells[0, m : m + 1, span]
            code = (CAP + (cell & (CAP - 1))) << ((cell >> 7) & 3)
            code = jnp.where(cell >= 512, -code, code)
            meta = jnp.where(meta_row == m, code, 0).astype(F32)
            pieces.append(jnp.concatenate([vals, meta], axis=0).astype(BF16))
        stacked = jnp.concatenate(pieces, axis=0)
        if m == 0:
            loads[4].wait()
        for n in range(parts):
            want = order[0, m, :, n * LO : (n + 1) * LO]
            onehot = (sub == (want & (LO - 1))).astype(F32).astype(BF16)
            both = jnp.dot(stacked, onehot, preferred_element_type=F32)
            part = want >> 8
            got = both[:high]
            for h in range(1, parts):
                got = jnp.where(part == h, both[h * high : (h + 1) * high], got)
            listed[m, 2 * n] = got[:, :CAP]
            listed[m, 2 * n + 1] = got[:, CAP:]
        listed[m, 2 * parts] = jnp.zeros((high, CAP), F32)
        listed[m, 2 * parts + 1] = jnp.zeros((high, CAP), F32)
    loads[6].wait()

    slots = wire.reshape(tiles, 2 * width + 2, CAP)
    lane = lax.broadcasted_iota(jnp.int32, (high, CAP), 1)
    meta_lane = lax.broadcasted_iota(jnp.int32, (META, CAP), 1)
    meta_sub = lax.broadcasted_iota(jnp.int32, (META, CAP), 0)

    def window(m, start):
        base = start >> 7
        shift = start & (CAP - 1)
        back = (CAP - shift) & (CAP - 1)
        near = pltpu.roll(listed[m, base], back, 1)
        far = pltpu.roll(listed[m, base + 1], back, 1)
        return jnp.where(lane < CAP - shift, near, far)

    starts = [jnp.int32(0), jnp.int32(0)]
    for q in range(tiles):
        sizes = [counts[0, m, 0, q] for m in range(2)]
        got = [window(m, starts[m]) for m in range(2)]
        meta = [jnp.where(meta_lane < sizes[m], got[m][width:], 0.0) for m in range(2)]
        meta = jnp.where(meta_sub == 0, meta[0], meta[1])
        block = jnp.concatenate([got[0][:width], got[1][:width], meta], axis=0)
        slots[q] = block.astype(BF16)[: 2 * width + 2]
        starts = [starts[m] + sizes[m] for m in range(2)]


def scatter(wire, m, width):
    tiles = wire.shape[0]
    slots = wire.reshape(tiles, 2 * width + 2, CAP)
    group = 4
    lanes = group * CAP
    low = lax.broadcasted_iota(jnp.int32, (LO, lanes), 0)
    total = None
    for s in range(0, tiles, group):
        vals = [slots[s + i, m * width : (m + 1) * width, :].astype(F32) for i in range(group)]
        meta = [slots[s + i, 2 * width : 2 * width + 2, :].astype(F32) for i in range(group)]
        vals = jnp.concatenate(vals, axis=1)
        code = jnp.concatenate(meta, axis=1)[m : m + 1].astype(jnp.int32)
        size = jnp.abs(code)
        scale = sum((size >= CAP << k).astype(jnp.int32) for k in range(1, 4))
        cell = (size >> scale) - CAP + (scale << 7) + jnp.where(code < 0, 512, 0)
        cell = jnp.where(code == 0, -1, cell)
        cell_hi = cell >> 8
        cell_lo = cell & (LO - 1)
        split = [jnp.where(cell_hi == h, vals, 0.0) for h in range(4)]
        left = jnp.concatenate(split, axis=0).astype(BF16)
        right = (low == cell_lo).astype(F32).astype(BF16)
        part = lax.dot_general(left, right, NT, preferred_element_type=F32)
        total = part if total is None else total + part
    return total


def mixed_kernel(wire, first_step, mix_t, mixed, west, east):
    width = mix_t.shape[0]
    total = scatter(wire, 1, width)
    mix = mix_t[...]
    mix_hi = mix.astype(BF16)
    mix_lo = (mix - mix_hi.astype(F32)).astype(BF16)
    for h in range(4):
        start = jnp.concatenate([first_step[2 * h], first_step[2 * h + 1]], axis=1)
        field = total[h * width : (h + 1) * width] - start
        field_hi = field.astype(BF16)
        field_lo = (field - field_hi.astype(F32)).astype(BF16)
        out = jnp.dot(mix_hi, field_hi, preferred_element_type=F32)
        out += jnp.dot(mix_hi, field_lo, preferred_element_type=F32)
        out += jnp.dot(mix_lo, field_hi, preferred_element_type=F32)
        mixed[2 * h] = out[:, :CAP]
        mixed[2 * h + 1] = out[:, CAP:]
        if h == 0:
            west[...] = out[:, :CAP]
        if h == 3:
            east[...] = out[:, CAP:]


def direct_kernel(wire, multiplier, mixed, diag, side, base):
    lons, width, lats = multiplier.shape
    total = scatter(wire, 0, width)
    lane = lax.broadcasted_iota(jnp.int32, (width, lats), 1)
    for i in range(lons):
        h, half = i // 2, (i % 2) * CAP
        part = total[h * width : (h + 1) * width, half : half + CAP]
        here = mixed[i]
        beside = jnp.where(lane == lats - 1, 0.0, pltpu.roll(here, lats - 1, 1))
        beside += jnp.where(lane == 0, 0.0, pltpu.roll(here, 1, 1))
        if i:
            beside += mixed[i - 1]
        if i + 1 < lons:
            beside += mixed[i + 1]
        base[i] = multiplier[i] + part + diag[i] * here + side[i] * beside


def final_kernel(base, west, east, side, out):
    lons = base.shape[0]
    rows = [base[i] for i in range(lons)]
    rows[0] += side[0] * west[...]
    rows[-1] += side[lons - 1] * east[...]
    out[...] = jnp.stack(rows, axis=1)


def halo(first, last):
    count = lax.axis_size("tile")
    up = [(i, (i + 1) % count) for i in range(count)]
    down = [(j, i) for i, j in up]
    return lax.ppermute(last, "tile", up), lax.ppermute(first, "tile", down)


def local(
    multiplier,
    coef_diag,
    coef_side,
    mixing,
    jacobians,
    departures,
    counts,
    row_order,
    obs_cell,
    obs_block,
):
    tiles = lax.axis_size("tile")
    _, width, lons, lats = multiplier.shape
    rows = departures.shape[2]
    wire = pl.pallas_call(
        pack_kernel,
        out_shape=jax.ShapeDtypeStruct((tiles, width + 1, 2, CAP), BF16),
        in_specs=[HBM] * 6,
        out_specs=VMEM,
        scratch_shapes=[
            pltpu.SMEM(counts.shape, jnp.int32),
            pltpu.VMEM(departures.shape[1:], BF16),
            pltpu.VMEM(row_order.shape, jnp.int32),
            pltpu.VMEM(obs_cell.shape, jnp.int32),
            pltpu.VMEM(obs_block.shape, jnp.int32),
            pltpu.VMEM(jacobians.shape, BF16),
            pltpu.VMEM((2, rows // CAP + 2, width + META, CAP), F32),
            pltpu.SemaphoreType.DMA((7,)),
        ],
        compiler_params=PACK_PARAMS,
        name="pack",
    )(counts, departures, row_order, obs_cell, obs_block, jacobians)
    wire, multiplier, coef_diag, coef_side, mixing = lax.optimization_barrier(
        (wire, multiplier, coef_diag, coef_side, mixing)
    )
    received = lax.all_to_all(wire, "tile", split_axis=0, concat_axis=0, tiled=True)

    mult_t = multiplier[0].transpose(1, 0, 2)
    diag_t = coef_diag[0].transpose(1, 0, 2)
    side_t = coef_side[0].transpose(1, 0, 2)
    mix_t = mixing.T
    windows = lax.axis_size("win")
    following = lax.ppermute(
        mult_t.astype(BF16), "win", [(i, i - 1) for i in range(1, windows)]
    ).astype(F32)
    mixed = jnp.einsum("cd,xcy->xdy", mixing, following, precision=lax.Precision.HIGHEST)
    west, east = halo(mixed[0], mixed[-1])
    rimmed = jnp.concatenate([west[None], mixed, east[None]], axis=0)
    padded = jnp.pad(mixed, ((0, 0), (0, 0), (1, 1)))
    beside = rimmed[2:] + rimmed[:-2] + padded[:, :, 2:] + padded[:, :, :-2]
    first_step = diag_t * mixed + side_t * beside

    field = jax.ShapeDtypeStruct((lons, width, lats), F32)
    edge = jax.ShapeDtypeStruct((width, lats), F32)
    mixed, first, last = pl.pallas_call(
        mixed_kernel,
        out_shape=(field, edge, edge),
        in_specs=[VMEM] * 3,
        out_specs=(VMEM,) * 3,
        compiler_params=PARAMS,
        name="mix",
    )(received, first_step, mix_t)
    west, east = halo(first, last)
    base = pl.pallas_call(
        direct_kernel,
        out_shape=field,
        in_specs=[VMEM] * 5,
        out_specs=VMEM,
        compiler_params=PARAMS,
        name="direct",
    )(received, mult_t, mixed, diag_t, side_t)
    out = pl.pallas_call(
        final_kernel,
        out_shape=jax.ShapeDtypeStruct((width, lons, lats), F32),
        in_specs=[VMEM] * 4,
        out_specs=VMEM,
        compiler_params=PARAMS,
        name="final",
    )(base, west, east, side_t)
    return out[None]


def solution(mesh):
    in_specs = (
        P("win", None, "tile", None),
        P("win", None, "tile", None),
        P("win", None, "tile", None),
        P(),
        P(),
        P("win", None, "tile", None),
        P("win", None, "tile", None),
        P("win", None, "tile", None),
        P("win", None, "tile"),
        P("win", None, "tile"),
    )
    out_specs = P("win", None, "tile", None)
    return jax.shard_map(local, mesh=mesh, in_specs=in_specs, out_specs=out_specs, check_vma=False)
```

```python
import jax
import jax.numpy as jnp
from jax import lax
from jax.experimental import pallas as pl
from jax.experimental.pallas import tpu as pltpu
from jax.sharding import PartitionSpec as P

CAP = 128
LO = 256
META = 8
OUT = 8
F32 = jnp.float32
BF16 = jnp.bfloat16
NT = (((1,), (1,)), ((), ()))
VMEM = pl.BlockSpec(memory_space=pltpu.VMEM)
HBM = pl.BlockSpec(memory_space=pltpu.HBM)
SMEM = pl.BlockSpec(memory_space=pltpu.SMEM)
PARAMS = pltpu.CompilerParams(vmem_limit_bytes=48 * 2**20)
PACK_PARAMS = pltpu.CompilerParams(vmem_limit_bytes=60 * 2**20)


def pack_kernel(
    counts_hbm,
    deps_hbm,
    order_hbm,
    cells_hbm,
    blocks_hbm,
    jac_hbm,
    wire_hbm,
    counts,
    deps,
    order,
    cells,
    blocks,
    jac,
    listed0,
    listed1,
    codes,
    wire,
    sems,
):
    loads = [
        pltpu.make_async_copy(jac_hbm, jac, sems.at[0]),
        pltpu.make_async_copy(blocks_hbm, blocks, sems.at[1]),
        pltpu.make_async_copy(cells_hbm, cells, sems.at[2]),
        pltpu.make_async_copy(deps_hbm.at[0, 0], deps.at[0], sems.at[3]),
        pltpu.make_async_copy(order_hbm, order, sems.at[4]),
        pltpu.make_async_copy(deps_hbm.at[0, 1], deps.at[1], sems.at[5]),
        pltpu.make_async_copy(counts_hbm, counts, sems.at[6]),
    ]
    for load in loads:
        load.start()
    kinds, width, _ = jac.shape
    tiles = wire_hbm.shape[0]
    rows = deps.shape[1]
    parts = rows // LO
    high = width + META
    slots = wire.reshape(tiles, 2 * width + 2, CAP)
    meta_row = lax.broadcasted_iota(jnp.int32, (META, LO), 0)
    sub = lax.broadcasted_iota(jnp.int32, (LO, LO), 0).astype(F32).astype(BF16)
    one, zero = jnp.ones((), BF16), jnp.zeros((), BF16)
    lane = lax.broadcasted_iota(jnp.int32, (high, CAP), 1)
    lane_row = lax.broadcasted_iota(jnp.int32, (2, CAP), 1)
    for load in loads[:4]:
        load.wait()
    half = kinds // 2
    jac_pair = [jnp.concatenate([jac[b], jac[b + half]], axis=1).astype(F32) for b in range(half)]
    jac_pair = jnp.concatenate(jac_pair, axis=0).astype(BF16)

    def in_list_order(m, listed):
        pieces = []
        for j in range(parts):
            span = slice(j * LO, (j + 1) * LO)
            kind = blocks[0, m : m + 1, span]
            dep = deps[m, span, :].T
            low_kind = jnp.where(kind < half, 1.0, 0.0)
            dep = jnp.concatenate(
                [dep * low_kind.astype(BF16), dep * (1.0 - low_kind).astype(BF16)], axis=0
            )
            prod = jnp.dot(jac_pair, dep, preferred_element_type=F32)
            kind = kind & (half - 1)
            vals = prod[:width]
            for b in range(1, half):
                vals = jnp.where(kind == b, prod[b * width : (b + 1) * width], vals)
            cell = cells[0, m : m + 1, span]
            code = (CAP + (cell & (CAP - 1))) << ((cell >> 7) & 3)
            code = jnp.where(cell >= 512, -code, code)
            meta = jnp.where(meta_row == m, code, 0).astype(F32)
            pieces.append(jnp.concatenate([vals, meta], axis=0).astype(BF16))
        stacked = jnp.concatenate(pieces, axis=0)
        if m == 0:
            loads[4].wait()
        for n in range(parts):
            want = order[0, m, :, n * LO : (n + 1) * LO]
            onehot = jnp.where(sub == (want & (LO - 1)).astype(F32).astype(BF16), one, zero)
            both = jnp.dot(stacked, onehot, preferred_element_type=F32)
            part = want >> 8
            got = both[:high]
            for h in range(1, parts):
                got = jnp.where(part == h, both[h * high : (h + 1) * high], got)
            listed[2 * n] = got[:, :CAP].astype(BF16)
            listed[2 * n + 1] = got[:, CAP:].astype(BF16)
        listed[2 * parts] = jnp.zeros((high, CAP), BF16)
        listed[2 * parts + 1] = jnp.zeros((high, CAP), BF16)

    def window(listed, start):
        base = start >> 7
        shift = start & (CAP - 1)
        back = (CAP - shift) & (CAP - 1)
        near = pltpu.roll(listed[base], back, 1)
        far = pltpu.roll(listed[base + 1], back, 1)
        return jnp.where(lane < CAP - shift, near, far)

    in_list_order(0, listed0)
    loads[6].wait()
    start = jnp.int32(0)
    for q in range(tiles):
        size = counts[0, 0, 0, q]
        got = window(listed0, start)
        slots[q, :width] = got[:width]
        code = got[width : width + 2]
        codes[q] = jnp.where(lane_row < size, code.astype(F32), 0.0)
        start += size
    loads[5].wait()
    in_list_order(1, listed1)
    start = jnp.int32(0)
    stores = []
    for q in range(tiles):
        size = counts[0, 1, 0, q]
        got = window(listed1, start)
        slots[q, width : 2 * width] = got[:width]
        code = jnp.where(lane_row < size, got[width : width + 2].astype(F32), 0.0)
        slots[q, 2 * width :] = (codes[q] + code).astype(BF16)
        start += size
        if (q + 1) % OUT == 0:
            k = q // OUT
            span = pl.ds(k * OUT, OUT)
            store = pltpu.make_async_copy(wire.at[span], wire_hbm.at[span], sems.at[7 + k])
            store.start()
            stores.append(store)
    for store in stores:
        store.wait()


def scatter(wire, m, width):
    tiles = wire.shape[0]
    slots = wire.reshape(tiles, 2 * width + 2, CAP)
    group = 4
    lanes = group * CAP
    high = width + META
    first = m * (width - META)
    low = lax.broadcasted_iota(jnp.int32, (LO, lanes), 0).astype(F32).astype(BF16)
    one, zero = jnp.ones((), BF16), jnp.zeros((), BF16)
    total = None
    for s in range(0, tiles, group):
        vals = [slots[s + i, first : first + high, :] for i in range(group)]
        meta = [slots[s + i, 2 * width : 2 * width + 2, :].astype(F32) for i in range(group)]
        vals = jnp.concatenate(vals, axis=1)
        code = jnp.concatenate(meta, axis=1)[m : m + 1].astype(jnp.int32)
        size = jnp.abs(code)
        scale = sum((size >= CAP << k).astype(jnp.int32) for k in range(1, 4))
        cell = (size >> scale) - CAP + (scale << 7) + jnp.where(code < 0, 512, 0)
        cell = jnp.where(code == 0, -1, cell)
        cell_hi = cell >> 8
        cell_lo = (cell & (LO - 1)).astype(F32).astype(BF16)
        split = [vals * (cell_hi == h).astype(F32).astype(BF16) for h in range(4)]
        left = jnp.concatenate(split, axis=0)
        right = jnp.where(low == cell_lo, one, zero)
        part = lax.dot_general(left, right, NT, preferred_element_type=F32)
        total = part if total is None else total + part
    skip = m * META
    return [total[h * high + skip : h * high + skip + width] for h in range(4)]


def mixed_kernel(wire, first_step, mix_t, mixed, west, east):
    width = mix_t.shape[0]
    total = scatter(wire, 1, width)
    mix = mix_t[...]
    mix_hi = mix.astype(BF16)
    mix_lo = (mix - mix_hi.astype(F32)).astype(BF16)
    for h in range(4):
        start = jnp.concatenate([first_step[2 * h], first_step[2 * h + 1]], axis=1)
        field = total[h] - start
        field_hi = field.astype(BF16)
        field_lo = (field - field_hi.astype(F32)).astype(BF16)
        out = jnp.dot(mix_hi, field_hi, preferred_element_type=F32)
        out += jnp.dot(mix_hi, field_lo, preferred_element_type=F32)
        out += jnp.dot(mix_lo, field_hi, preferred_element_type=F32)
        mixed[2 * h] = out[:, :CAP]
        mixed[2 * h + 1] = out[:, CAP:]
        if h == 0:
            west[...] = out[:, :CAP]
        if h == 3:
            east[...] = out[:, CAP:]


def direct_kernel(wire, multiplier, mixed, diag, side, base):
    lons, width, lats = multiplier.shape
    total = scatter(wire, 0, width)
    lane = lax.broadcasted_iota(jnp.int32, (width, lats), 1)
    for i in range(lons):
        h, half = i // 2, (i % 2) * CAP
        part = total[h][:, half : half + CAP]
        here = mixed[i]
        beside = jnp.where(lane == lats - 1, 0.0, pltpu.roll(here, lats - 1, 1))
        beside += jnp.where(lane == 0, 0.0, pltpu.roll(here, 1, 1))
        if i:
            beside += mixed[i - 1]
        if i + 1 < lons:
            beside += mixed[i + 1]
        base[i] = multiplier[i] + part + diag[i] * here + side[i] * beside


def final_kernel(base, west, east, side, out):
    lons = base.shape[0]
    rows = [base[i] for i in range(lons)]
    rows[0] += side[0] * west[...]
    rows[-1] += side[lons - 1] * east[...]
    out[...] = jnp.stack(rows, axis=1)


def halo(first, last):
    count = lax.axis_size("tile")
    up = [(i, (i + 1) % count) for i in range(count)]
    down = [(j, i) for i, j in up]
    return lax.ppermute(last, "tile", up), lax.ppermute(first, "tile", down)


def local(
    multiplier,
    coef_diag,
    coef_side,
    mixing,
    jacobians,
    departures,
    counts,
    row_order,
    obs_cell,
    obs_block,
):
    tiles = lax.axis_size("tile")
    _, width, lons, lats = multiplier.shape
    rows = departures.shape[2]
    wire = pl.pallas_call(
        pack_kernel,
        out_shape=jax.ShapeDtypeStruct((tiles, width + 1, 2, CAP), BF16),
        in_specs=[HBM] * 6,
        out_specs=HBM,
        scratch_shapes=[
            pltpu.SMEM(counts.shape, jnp.int32),
            pltpu.VMEM(departures.shape[1:], BF16),
            pltpu.VMEM(row_order.shape, jnp.int32),
            pltpu.VMEM(obs_cell.shape, jnp.int32),
            pltpu.VMEM(obs_block.shape, jnp.int32),
            pltpu.VMEM(jacobians.shape, BF16),
            pltpu.VMEM((rows // CAP + 2, width + META, CAP), BF16),
            pltpu.VMEM((rows // CAP + 2, width + META, CAP), BF16),
            pltpu.VMEM((tiles, 2, CAP), F32),
            pltpu.VMEM((tiles, width + 1, 2, CAP), BF16),
            pltpu.SemaphoreType.DMA((7 + tiles // OUT,)),
        ],
        compiler_params=PACK_PARAMS,
        name="pack",
    )(counts, departures, row_order, obs_cell, obs_block, jacobians)
    wire, multiplier, coef_diag, coef_side, mixing = lax.optimization_barrier(
        (wire, multiplier, coef_diag, coef_side, mixing)
    )
    received = lax.all_to_all(wire, "tile", split_axis=0, concat_axis=0, tiled=True)

    mult_t = multiplier[0].transpose(1, 0, 2)
    diag_t = coef_diag[0].transpose(1, 0, 2)
    side_t = coef_side[0].transpose(1, 0, 2)
    mix_t = mixing.T
    windows = lax.axis_size("win")
    following = lax.ppermute(
        mult_t.astype(BF16), "win", [(i, i - 1) for i in range(1, windows)]
    ).astype(F32)
    mixed = jnp.einsum("cd,xcy->xdy", mixing, following, precision=lax.Precision.HIGHEST)
    west, east = halo(mixed[0], mixed[-1])
    rimmed = jnp.concatenate([west[None], mixed, east[None]], axis=0)
    padded = jnp.pad(mixed, ((0, 0), (0, 0), (1, 1)))
    beside = rimmed[2:] + rimmed[:-2] + padded[:, :, 2:] + padded[:, :, :-2]
    first_step = diag_t * mixed + side_t * beside

    field = jax.ShapeDtypeStruct((lons, width, lats), F32)
    edge = jax.ShapeDtypeStruct((width, lats), F32)
    mixed, first, last = pl.pallas_call(
        mixed_kernel,
        out_shape=(field, edge, edge),
        in_specs=[VMEM] * 3,
        out_specs=(VMEM,) * 3,
        compiler_params=PARAMS,
        name="mix",
    )(received, first_step, mix_t)
    west, east = halo(first, last)
    base = pl.pallas_call(
        direct_kernel,
        out_shape=field,
        in_specs=[VMEM] * 5,
        out_specs=VMEM,
        compiler_params=PARAMS,
        name="direct",
    )(received, mult_t, mixed, diag_t, side_t)
    out = pl.pallas_call(
        final_kernel,
        out_shape=jax.ShapeDtypeStruct((width, lons, lats), F32),
        in_specs=[VMEM] * 4,
        out_specs=VMEM,
        compiler_params=PARAMS,
        name="final",
    )(base, west, east, side_t)
    return out[None]


def solution(mesh):
    in_specs = (
        P("win", None, "tile", None),
        P("win", None, "tile", None),
        P("win", None, "tile", None),
        P(),
        P(),
        P("win", None, "tile", None),
        P("win", None, "tile", None),
        P("win", None, "tile", None),
        P("win", None, "tile"),
        P("win", None, "tile"),
    )
    out_specs = P("win", None, "tile", None)
    return jax.shard_map(local, mesh=mesh, in_specs=in_specs, out_specs=out_specs, check_vma=False)
```

```python
import jax
import jax.numpy as jnp
from jax import lax
from jax.experimental import pallas as pl
from jax.experimental.pallas import tpu as pltpu
from jax.sharding import PartitionSpec as P

CAP = 128
LO = 256
META = 8
OUT = 8
PART = 24
F32 = jnp.float32
BF16 = jnp.bfloat16
NT = (((1,), (1,)), ((), ()))
VMEM = pl.BlockSpec(memory_space=pltpu.VMEM)
HBM = pl.BlockSpec(memory_space=pltpu.HBM)
SMEM = pl.BlockSpec(memory_space=pltpu.SMEM)
PARAMS = pltpu.CompilerParams(vmem_limit_bytes=48 * 2**20)
PACK_PARAMS = pltpu.CompilerParams(vmem_limit_bytes=60 * 2**20)


def pack_kernel(
    counts_hbm,
    deps_hbm,
    order_hbm,
    cells_hbm,
    blocks_hbm,
    jac_hbm,
    wire_hbm,
    counts,
    deps,
    order,
    cells,
    blocks,
    jac,
    listed0,
    listed1,
    codes,
    wire,
    sems,
):
    loads = [
        pltpu.make_async_copy(jac_hbm, jac, sems.at[0]),
        pltpu.make_async_copy(blocks_hbm, blocks, sems.at[1]),
        pltpu.make_async_copy(cells_hbm, cells, sems.at[2]),
        pltpu.make_async_copy(deps_hbm.at[0, 0], deps.at[0], sems.at[3]),
        pltpu.make_async_copy(order_hbm, order, sems.at[4]),
        pltpu.make_async_copy(deps_hbm.at[0, 1], deps.at[1], sems.at[5]),
        pltpu.make_async_copy(counts_hbm, counts, sems.at[6]),
    ]
    for load in loads:
        load.start()
    kinds, width, _ = jac.shape
    tiles = wire_hbm.shape[0]
    rows = deps.shape[1]
    parts = rows // LO
    high = width + META
    slots = wire.reshape(tiles, 2 * width + 2, CAP)
    meta_row = lax.broadcasted_iota(jnp.int32, (META, LO), 0)
    sub = lax.broadcasted_iota(jnp.int32, (LO, LO), 0).astype(F32).astype(BF16)
    one, zero = jnp.ones((), BF16), jnp.zeros((), BF16)
    lane = lax.broadcasted_iota(jnp.int32, (high, CAP), 1)
    lane_row = lax.broadcasted_iota(jnp.int32, (2, CAP), 1)
    for load in loads[:4]:
        load.wait()
    half = kinds // 2
    jac_pair = [jnp.concatenate([jac[b], jac[b + half]], axis=1).astype(F32) for b in range(half)]
    jac_pair = jnp.concatenate(jac_pair, axis=0).astype(BF16)

    def in_list_order(m, listed):
        pieces = []
        for j in range(parts):
            span = slice(j * LO, (j + 1) * LO)
            kind = blocks[0, m : m + 1, span]
            dep = deps[m, span, :].T
            low_kind = jnp.where(kind < half, 1.0, 0.0)
            dep = jnp.concatenate(
                [dep * low_kind.astype(BF16), dep * (1.0 - low_kind).astype(BF16)], axis=0
            )
            prod = jnp.dot(jac_pair, dep, preferred_element_type=F32)
            kind = kind & (half - 1)
            vals = prod[:width]
            for b in range(1, half):
                vals = jnp.where(kind == b, prod[b * width : (b + 1) * width], vals)
            cell = cells[0, m : m + 1, span]
            code = (CAP + (cell & (CAP - 1))) << ((cell >> 7) & 3)
            code = jnp.where(cell >= 512, -code, code)
            meta = jnp.where(meta_row == m, code, 0).astype(F32)
            pieces.append(jnp.concatenate([vals, meta], axis=0).astype(BF16))
        stacked = jnp.concatenate(pieces, axis=0)
        if m == 0:
            loads[4].wait()
        for n in range(parts):
            want = order[0, m, :, n * LO : (n + 1) * LO]
            onehot = jnp.where(sub == (want & (LO - 1)).astype(F32).astype(BF16), one, zero)
            both = jnp.dot(stacked, onehot, preferred_element_type=F32)
            part = want >> 8
            got = both[:high]
            for h in range(1, parts):
                got = jnp.where(part == h, both[h * high : (h + 1) * high], got)
            listed[2 * n] = got[:, :CAP].astype(BF16)
            listed[2 * n + 1] = got[:, CAP:].astype(BF16)
        listed[2 * parts] = jnp.zeros((high, CAP), BF16)
        listed[2 * parts + 1] = jnp.zeros((high, CAP), BF16)

    def window(listed, start):
        base = start >> 7
        shift = start & (CAP - 1)
        back = (CAP - shift) & (CAP - 1)
        near = pltpu.roll(listed[base], back, 1)
        far = pltpu.roll(listed[base + 1], back, 1)
        return jnp.where(lane < CAP - shift, near, far)

    in_list_order(0, listed0)
    loads[6].wait()
    start = jnp.int32(0)
    for q in range(tiles):
        size = counts[0, 0, 0, q]
        got = window(listed0, start)
        slots[q, :width] = got[:width]
        code = got[width : width + 2]
        codes[q] = jnp.where(lane_row < size, code.astype(F32), 0.0)
        start += size
    loads[5].wait()
    in_list_order(1, listed1)
    start = jnp.int32(0)
    stores = []
    for q in range(tiles):
        size = counts[0, 1, 0, q]
        got = window(listed1, start)
        slots[q, width : 2 * width] = got[:width]
        code = jnp.where(lane_row < size, got[width : width + 2].astype(F32), 0.0)
        slots[q, 2 * width :] = (codes[q] + code).astype(BF16)
        start += size
        if (q + 1) % OUT == 0:
            k = q // OUT
            span = pl.ds(k * OUT, OUT)
            store = pltpu.make_async_copy(wire.at[span], wire_hbm.at[span], sems.at[7 + k])
            store.start()
            stores.append(store)
    for store in stores:
        store.wait()


def scatter(wire, m, width):
    tiles = wire.shape[0]
    slots = wire.reshape(tiles, 2 * width + 2, CAP)
    group = 4
    lanes = group * CAP
    high = width + META
    first = m * (width - META)
    low = lax.broadcasted_iota(jnp.int32, (LO, lanes), 0).astype(F32).astype(BF16)
    one, zero = jnp.ones((), BF16), jnp.zeros((), BF16)
    total = None
    for s in range(0, tiles, group):
        vals = [slots[s + i, first : first + high, :] for i in range(group)]
        meta = [slots[s + i, 2 * width : 2 * width + 2, :].astype(F32) for i in range(group)]
        vals = jnp.concatenate(vals, axis=1)
        code = jnp.concatenate(meta, axis=1)[m : m + 1].astype(jnp.int32)
        size = jnp.abs(code)
        scale = sum((size >= CAP << k).astype(jnp.int32) for k in range(1, 4))
        cell = (size >> scale) - CAP + (scale << 7) + jnp.where(code < 0, 512, 0)
        cell = jnp.where(code == 0, -1, cell)
        cell_hi = cell >> 8
        cell_lo = (cell & (LO - 1)).astype(F32).astype(BF16)
        split = [vals * (cell_hi == h).astype(F32).astype(BF16) for h in range(4)]
        left = jnp.concatenate(split, axis=0)
        right = jnp.where(low == cell_lo, one, zero)
        part = lax.dot_general(left, right, NT, preferred_element_type=F32)
        total = part if total is None else total + part
    skip = m * META
    return [total[h * high + skip : h * high + skip + width] for h in range(4)]


def mixed_kernel(wire, first_step, mix_t, mixed, west, east):
    width = mix_t.shape[0]
    total = scatter(wire, 1, width)
    mix = mix_t[...]
    mix_hi = mix.astype(BF16)
    mix_lo = (mix - mix_hi.astype(F32)).astype(BF16)
    for h in range(4):
        start = jnp.concatenate([first_step[2 * h], first_step[2 * h + 1]], axis=1)
        field = total[h] - start
        field_hi = field.astype(BF16)
        field_lo = (field - field_hi.astype(F32)).astype(BF16)
        out = jnp.dot(mix_hi, field_hi, preferred_element_type=F32)
        out += jnp.dot(mix_hi, field_lo, preferred_element_type=F32)
        out += jnp.dot(mix_lo, field_hi, preferred_element_type=F32)
        mixed[2 * h] = out[:, :CAP]
        mixed[2 * h + 1] = out[:, CAP:]
        if h == 0:
            west[...] = out[:, :CAP]
        if h == 3:
            east[...] = out[:, CAP:]


def direct_kernel(wire, multiplier, mixed, diag, side, base):
    lons, width, lats = multiplier.shape
    total = scatter(wire, 0, width)
    lane = lax.broadcasted_iota(jnp.int32, (width, lats), 1)
    rows = []
    for i in range(lons):
        h, half = i // 2, (i % 2) * CAP
        part = total[h][:, half : half + CAP]
        here = mixed[i]
        beside = jnp.where(lane == lats - 1, 0.0, pltpu.roll(here, lats - 1, 1))
        beside += jnp.where(lane == 0, 0.0, pltpu.roll(here, 1, 1))
        if i:
            beside += mixed[i - 1]
        if i + 1 < lons:
            beside += mixed[i + 1]
        rows.append(multiplier[i] + part + diag[i] * here + side[i] * beside)
    base[...] = jnp.stack(rows, axis=1)


def final_kernel(base, west, east, side, out_hbm, out, sems):
    width, lons, lats = base.shape
    count = width // PART
    none = [jnp.zeros((PART, lats), F32)] * (lons - 2)
    stores = []
    for k in range(count):
        span = pl.ds(k * PART, PART)
        first = side[0, span] * west[span]
        last = side[lons - 1, span] * east[span]
        out[span] = base[span] + jnp.stack([first] + none + [last], axis=1)
        store = pltpu.make_async_copy(out.at[span], out_hbm.at[span], sems.at[k])
        store.start()
        stores.append(store)
    for store in stores:
        store.wait()


def halo(first, last):
    count = lax.axis_size("tile")
    up = [(i, (i + 1) % count) for i in range(count)]
    down = [(j, i) for i, j in up]
    return lax.ppermute(last, "tile", up), lax.ppermute(first, "tile", down)


def local(
    multiplier,
    coef_diag,
    coef_side,
    mixing,
    jacobians,
    departures,
    counts,
    row_order,
    obs_cell,
    obs_block,
):
    tiles = lax.axis_size("tile")
    _, width, lons, lats = multiplier.shape
    rows = departures.shape[2]
    wire = pl.pallas_call(
        pack_kernel,
        out_shape=jax.ShapeDtypeStruct((tiles, width + 1, 2, CAP), BF16),
        in_specs=[HBM] * 6,
        out_specs=HBM,
        scratch_shapes=[
            pltpu.SMEM(counts.shape, jnp.int32),
            pltpu.VMEM(departures.shape[1:], BF16),
            pltpu.VMEM(row_order.shape, jnp.int32),
            pltpu.VMEM(obs_cell.shape, jnp.int32),
            pltpu.VMEM(obs_block.shape, jnp.int32),
            pltpu.VMEM(jacobians.shape, BF16),
            pltpu.VMEM((rows // CAP + 2, width + META, CAP), BF16),
            pltpu.VMEM((rows // CAP + 2, width + META, CAP), BF16),
            pltpu.VMEM((tiles, 2, CAP), F32),
            pltpu.VMEM((tiles, width + 1, 2, CAP), BF16),
            pltpu.SemaphoreType.DMA((7 + tiles // OUT,)),
        ],
        compiler_params=PACK_PARAMS,
        name="pack",
    )(counts, departures, row_order, obs_cell, obs_block, jacobians)
    wire, multiplier, coef_diag, coef_side, mixing = lax.optimization_barrier(
        (wire, multiplier, coef_diag, coef_side, mixing)
    )
    received = lax.all_to_all(wire, "tile", split_axis=0, concat_axis=0, tiled=True)

    mult_t = multiplier[0].transpose(1, 0, 2)
    diag_t = coef_diag[0].transpose(1, 0, 2)
    side_t = coef_side[0].transpose(1, 0, 2)
    mix_t = mixing.T
    windows = lax.axis_size("win")
    following = lax.ppermute(
        mult_t.astype(BF16), "win", [(i, i - 1) for i in range(1, windows)]
    ).astype(F32)
    mixed = jnp.einsum("cd,xcy->xdy", mixing, following, precision=lax.Precision.HIGHEST)
    west, east = halo(mixed[0], mixed[-1])
    rimmed = jnp.concatenate([west[None], mixed, east[None]], axis=0)
    padded = jnp.pad(mixed, ((0, 0), (0, 0), (1, 1)))
    beside = rimmed[2:] + rimmed[:-2] + padded[:, :, 2:] + padded[:, :, :-2]
    first_step = diag_t * mixed + side_t * beside

    field = jax.ShapeDtypeStruct((lons, width, lats), F32)
    edge = jax.ShapeDtypeStruct((width, lats), F32)
    mixed, first, last = pl.pallas_call(
        mixed_kernel,
        out_shape=(field, edge, edge),
        in_specs=[VMEM] * 3,
        out_specs=(VMEM,) * 3,
        compiler_params=PARAMS,
        name="mix",
    )(received, first_step, mix_t)
    west, east = halo(first, last)
    base = pl.pallas_call(
        direct_kernel,
        out_shape=jax.ShapeDtypeStruct((width, lons, lats), F32),
        in_specs=[VMEM] * 5,
        out_specs=VMEM,
        compiler_params=PARAMS,
        name="direct",
    )(received, mult_t, mixed, diag_t, side_t)
    out = pl.pallas_call(
        final_kernel,
        out_shape=jax.ShapeDtypeStruct((width, lons, lats), F32),
        in_specs=[VMEM] * 4,
        out_specs=HBM,
        scratch_shapes=[
            pltpu.VMEM((width, lons, lats), F32),
            pltpu.SemaphoreType.DMA((width // PART,)),
        ],
        compiler_params=PARAMS,
        name="final",
    )(base, west, east, side_t)
    return out[None]


def solution(mesh):
    in_specs = (
        P("win", None, "tile", None),
        P("win", None, "tile", None),
        P("win", None, "tile", None),
        P(),
        P(),
        P("win", None, "tile", None),
        P("win", None, "tile", None),
        P("win", None, "tile", None),
        P("win", None, "tile"),
        P("win", None, "tile"),
    )
    out_specs = P("win", None, "tile", None)
    return jax.shard_map(local, mesh=mesh, in_specs=in_specs, out_specs=out_specs, check_vma=False)
```
